32 devices in a mesh: section: 2 (over core), dp: 4 (over z), expert: 4 (over y, x).
Axes of the slice: x: 2, y: 2, z: 4, core: 2. Of those that a mesh axis runs over, the one named last changes fastest.
Arguments:
- tokens: bfloat16 [2, 768, 3072], P('section', 'expert'), may hold values from -6 to 6
- expert_ids: int32 [2, 768, 2], P('section', 'expert'), may hold values from 0 to 7, all different within a row; in each aligned block of 192 rows (0 to 191, 192 to 383, ..., all dimensions but the last counted through in order) at most 72 rows name the same one
- gate_probs: float32 [2, 768, 2], P('section', 'expert'), may hold values from 0.2 to 1
- cotangent: bfloat16 [2, 768, 3072], P('section', 'expert'), may hold values from -6 to 6
- w_gate: bfloat16 [2, 8, 3072, 8192], P('section', 'expert', None, 'dp'), may hold values from -0.109375 to 0.109375
- w_up: bfloat16 [2, 8, 3072, 8192], P('section', 'expert', None, 'dp'), may hold values from -0.109375 to 0.109375
- w_down: bfloat16 [2, 8, 8192, 3072], P('section', 'expert', 'dp'), may hold values from -0.0625 to 0.0625
Outputs:
- moe_out: bfloat16 [2, 768, 3072], P('section', 'expert')
- grad_handoff: bfloat16 [2, 768, 3072], P('section', 'expert')
The draws below stay inside these ranges and needn't reach their ends.
Inputs may be any that keep to these rules, and one draw needn't show every extreme that they name: `expert_ids`: A token's two experts differ. Among the 192 tokens of one device (aligned blocks of a section's tokens) no expert is named more than 72 times, a bound that some block reaches.
All inputs are finite; a program needn't handle non-finite values.
Results may differ from the reference program's by a relative error of at most 0.013.
Values may be sent and summed in bfloat16 or wider, within the bound.
No kernel may reach another device: no remote copies, remote signals or barrier semaphores. Data moves between devices by JAX's collectives and lax.ppermute only.
A program may use at most 256 MiB of HBM per device.

```python
import math
import jax
import jax.numpy as jnp
import numpy as np
from jax import lax

D = 3072
FF = 8192
EXPERTS = 8
TOK_DEV = 192
CAP = 72
TOKENS = 768
N_DP = 4
N_EXPERT = 4


def steps_of(stream_key, shape, pieces, smallest, largest):
    loudness = 1.0
    for dim, shards_of in pieces:
        draws = jax.random.uniform(jax.random.fold_in(jax.random.fold_in(stream_key, 6), dim), (shards_of,), jnp.float32, smallest / len(pieces), largest / len(pieces))
        loudness = loudness * jnp.repeat(jnp.exp(draws), shape[dim] // shards_of).reshape((-1,) + (1,) * (len(shape) - 1 - dim))
    return loudness


def deal_out(own_key, own, number, rows, count, top, bound, skew):
    order = jax.random.permutation(own_key, count)
    packed, usual = load_shares(count, rows * top, bound, skew, True), load_shares(count, rows * top, bound, skew, False)
    places = jnp.arange(count)

    def named(tallies, offset_by):
        used = int((tallies > 0).sum())
        fixed = max(1, used // 4)
        moved = fixed + (places - fixed + offset_by * (used - fixed)) % max(1, count - fixed)
        return jnp.zeros((count,), jnp.int32).at[order[jnp.where(places < fixed, places, moved)]].set(jnp.asarray(tallies, jnp.int32))

    tallies = jnp.where(number % 4 == 0, named(packed, number // 4), named(usual, number - number // 4 - 1))
    mixed = jax.random.permutation(jax.random.fold_in(own, 3), count)
    source_of, taker = mixed[0:count // 2 * 2:2], mixed[1:count // 2 * 2:2]
    margin = jnp.minimum(tallies[source_of] - 1, bound - tallies[taker]) // 2
    margin = jnp.where((source_of == order[0]) | (taker == order[0]) | (tallies[taker] == 0), 0, jnp.maximum(margin, 0))
    moved = jax.random.randint(jax.random.fold_in(own, 4), (count // 2,), 0, 1 << 20) % (margin + 1)
    tallies = tallies.at[source_of].add(-moved).at[taker].add(moved)
    members = jnp.searchsorted(jnp.cumsum(tallies), jnp.arange(rows * top), side="right").astype(jnp.int32)
    grid = members.reshape(top, rows).T
    grid = grid[jax.random.permutation(jax.random.fold_in(own, 1), rows)]
    offset_by = jax.random.randint(jax.random.fold_in(own, 2), (rows, 1), 0, top)
    return jnp.take_along_axis(grid, (jnp.arange(top)[None, :] + offset_by) % top, axis=1)


def load_shares(count, total, limit, skew, full):
    weights = [(1 << 20) // math.isqrt(rank ** skew) + 1 for rank in range(1, count + 1)]
    largest = limit if full else min(limit, max(-(-total // count), total * weights[0] // sum(weights)))
    least = 1 if total - largest >= count - 1 else 0
    holding, rest = [largest] + [least] * (count - 1), total - largest - least * (count - 1)
    while rest > 0:
        free = [i for i in range(1, count) if holding[i] < largest] or [i for i in range(1, count) if holding[i] < limit]
        pool, budget = sum([weights[i] for i in free]), rest
        for i in free:
            extra = min(limit - holding[i], max(1, budget * weights[i] // pool), rest)
            holding[i] = holding[i] + extra
            rest = rest - extra
    return np.array(holding)


def normal_values(own_key, shape, scale, most, split=(), kind=jnp.bfloat16):
    gain = steps_of(own_key, shape, split, -0.22, 0.18) if split else 1.0
    array = jax.random.normal(own_key, shape, jnp.float32) * scale * gain
    return jnp.minimum(jnp.maximum(array, -most), most).astype(kind)


def setup_inputs(seed: int = 0) -> dict:
    key_of = jax.random.split(jax.random.key(seed), 8)
    tokens = normal_values(key_of[0], (2, TOKENS, D), 1.0, 6.0, ((0, 2), (1, 4)))
    expert_ids_keys = jax.random.split(jax.random.fold_in(key_of[1], 1), 2 * TOKENS // TOK_DEV)
    expert_ids_turns = jax.random.permutation(jax.random.fold_in(key_of[1], 3), 2 * TOKENS // TOK_DEV)
    expert_ids = jax.vmap(lambda own, number: deal_out(jax.random.fold_in(key_of[1], 2), own, number, TOK_DEV, EXPERTS, 2, CAP, 2))(expert_ids_keys, expert_ids_turns).reshape((2, TOKENS, 2))
    gate_probs = jnp.clip(0.2 + 0.8 * jax.random.uniform(key_of[2], (2, TOKENS, 2), jnp.float32) ** steps_of(key_of[2], (2, TOKENS, 2), ((0, 2), (1, 4)), -0.2, 0.2), 0.2, 1.0)
    cotangent = normal_values(key_of[3], (2, TOKENS, D), 1.0, 6.0, ((0, 2), (1, 4)))
    w_gate = normal_values(key_of[4], (2, EXPERTS, D, FF), D ** -0.5, 0.109375, ((0, 2), (1, 4), (3, 4)))
    w_up = normal_values(key_of[5], (2, EXPERTS, D, FF), D ** -0.5, 0.109375, ((0, 2), (1, 4), (3, 4)))
    w_down = normal_values(key_of[6], (2, EXPERTS, FF, D), FF ** -0.5, 0.0625, ((0, 2), (1, 4), (2, 4)))
    return dict(tokens=tokens, expert_ids=expert_ids, gate_probs=gate_probs, cotangent=cotangent, w_gate=w_gate, w_up=w_up, w_down=w_down)


def slot_tables(chosen, weights_two, experts, capacity):
    number = chosen.shape[0]
    flattened = chosen.reshape(-1)
    one_hot = (flattened[:, None] == jnp.arange(experts, dtype=jnp.int32)[None, :]).astype(jnp.int32)
    earlier = jnp.cumsum(one_hot, axis=0) - one_hot
    position = jnp.sum(earlier * one_hot, axis=1)
    slot_index = flattened * capacity + position
    selection = (slot_index[:, None] == jnp.arange(experts * capacity, dtype=jnp.int32)[None, :]).astype(jnp.float32)
    selection = selection.reshape(number, 2, experts * capacity)
    routing = jnp.sum(selection, axis=1)
    weighting = jnp.sum(selection * weights_two[:, :, None].astype(jnp.float32), axis=1)
    return routing, weighting


def expert_work(operands):
    slot_rows, cot_rows, gate_mat, up_mat, down_mat = operands
    gate = jnp.dot(slot_rows, gate_mat, preferred_element_type=jnp.float32)
    upper = jnp.dot(slot_rows, up_mat, preferred_element_type=jnp.float32)
    sigma = jax.nn.sigmoid(gate)
    active = gate * sigma
    slope = sigma * (1.0 + gate * (1.0 - sigma))
    hidden = (active * upper).astype(jnp.bfloat16)
    number = hidden.shape[0]
    hidden_panels = hidden.reshape(number, N_DP, FF // N_DP).astype(jnp.float32)
    down_panels = down_mat.reshape(N_DP, FF // N_DP, D).astype(jnp.float32)
    panel_out = jnp.einsum('rqf,qfd->rqd', hidden_panels, down_panels).astype(jnp.bfloat16)
    expert_out = jnp.sum(panel_out.astype(jnp.float32), axis=1)
    hidden_cot = jnp.dot(cot_rows, down_mat.T, preferred_element_type=jnp.float32)
    gate_cot = (hidden_cot * upper * slope).astype(jnp.bfloat16).reshape(number, N_DP, FF // N_DP).astype(jnp.float32)
    up_cot = (hidden_cot * active).astype(jnp.bfloat16).reshape(number, N_DP, FF // N_DP).astype(jnp.float32)
    gate_panels = gate_mat.reshape(D, N_DP, FF // N_DP).astype(jnp.float32)
    up_panels = up_mat.reshape(D, N_DP, FF // N_DP).astype(jnp.float32)
    panel_grad = jnp.einsum('rqf,dqf->rqd', gate_cot, gate_panels) + jnp.einsum('rqf,dqf->rqd', up_cot, up_panels)
    slot_grad = jnp.sum(panel_grad.astype(jnp.bfloat16).astype(jnp.float32), axis=1)
    return expert_out, slot_grad


def section_pass(activations, chosen, weights_two, upstream, gate_all, up_all, down_all):
    blocks = N_EXPERT
    grouped = activations.reshape(blocks, TOK_DEV, D).astype(jnp.float32)
    routing, weighting = jax.vmap(lambda one, two: slot_tables(one, two, EXPERTS, CAP))(
        chosen.reshape(blocks, TOK_DEV, 2), weights_two.reshape(blocks, TOK_DEV, 2))
    slot_rows = jnp.einsum('nts,ntd->nsd', routing, grouped, precision=lax.Precision.HIGHEST).astype(jnp.bfloat16)
    cot_rows = jnp.einsum('nts,ntd->nsd', weighting, upstream.reshape(blocks, TOK_DEV, D).astype(jnp.float32),
                          precision=lax.Precision.HIGHEST).astype(jnp.bfloat16)

    def by_expert(values):
        return values.reshape(blocks, EXPERTS, CAP, D).transpose(1, 0, 2, 3).reshape(EXPERTS, blocks * CAP, D)

    def by_block(values):
        return values.reshape(EXPERTS, blocks, CAP, D).transpose(1, 0, 2, 3).reshape(blocks, EXPERTS * CAP, D)

    expert_out, slot_grad = lax.map(expert_work, (by_expert(slot_rows), by_expert(cot_rows), gate_all, up_all, down_all))
    outputs = jnp.einsum('nts,nsd->ntd', weighting, by_block(expert_out), precision=lax.Precision.HIGHEST)
    gradient = jnp.einsum('nts,nsd->ntd', routing, by_block(slot_grad), precision=lax.Precision.HIGHEST)
    return outputs.astype(jnp.bfloat16).reshape(TOKENS, D), gradient.astype(jnp.bfloat16).reshape(TOKENS, D)


def reference(tokens, expert_ids, gate_probs, cotangent, w_gate, w_up, w_down):
    first_out, first_grad = section_pass(tokens[0], expert_ids[0], gate_probs[0], cotangent[0], w_gate[0], w_up[0], w_down[0])
    second_out, second_grad = section_pass(tokens[1], expert_ids[1], gate_probs[1], cotangent[1], w_gate[1], w_up[1], w_down[1])
    return jnp.stack([first_out, second_out]), jnp.stack([second_grad, first_grad])
```

```python
import jax
import jax.numpy as jnp
from jax import lax
from jax.sharding import PartitionSpec as P

CAP = 72
BF = jnp.bfloat16
F32 = jnp.float32


def swap(block, axis, flip):
    size = lax.axis_size(axis)
    return lax.ppermute(block, axis, [(i, i ^ flip) for i in range(size)])


def slot_tables(chosen, weights_two, experts, local, capacity, me):
    number = chosen.shape[0]
    relative = ((chosen // local) ^ me) * local + chosen % local
    flattened = relative.reshape(-1)
    one_hot = (flattened[:, None] == jnp.arange(experts, dtype=jnp.int32)[None, :]).astype(
        jnp.int32
    )
    earlier = jnp.cumsum(one_hot, axis=0) - one_hot
    position = jnp.sum(earlier * one_hot, axis=1)
    slot_index = flattened * capacity + position
    selection = (
        slot_index[:, None] == jnp.arange(experts * capacity, dtype=jnp.int32)[None, :]
    ).astype(F32)
    selection = selection.reshape(number, 2, experts * capacity)
    routing = jnp.sum(selection, axis=1)
    weighting = jnp.sum(selection * weights_two[:, :, None], axis=1)
    slot_weight = jnp.sum(weighting, axis=0)
    return routing, weighting, slot_weight


def dot(a, b, dims):
    return lax.dot_general(a, b, dims, preferred_element_type=F32)


def sum_over(block, axis):
    size = lax.axis_size(axis)
    if size != 4:
        return lax.psum(block, axis)
    half = block.shape[1] // 2
    z = lax.axis_index(axis)
    first = (z == 0) | (z == 3)
    left, right = block[:, :half], block[:, half:]
    mine = jnp.where(first, left, right)
    other = jnp.where(first, right, left)
    mine = mine.astype(F32) + swap(other, axis, 1).astype(F32)
    mine = mine.astype(BF)
    mine = (mine.astype(F32) + swap(mine, axis, 3).astype(F32)).astype(BF)
    other = swap(mine, axis, 1)
    return jnp.concatenate([jnp.where(first, mine, other), jnp.where(first, other, mine)], axis=1)


def body(tokens, expert_ids, gate_probs, cotangent, w_gate, w_up, w_down):
    activations, chosen, weights_two, upstream = tokens[0], expert_ids[0], gate_probs[0], cotangent[0]
    gate_local, up_local, down_local = w_gate[0], w_up[0], w_down[0]
    local = gate_local.shape[0]
    model = activations.shape[1]
    groups = lax.axis_size("expert")
    me = lax.axis_index("expert")
    experts = local * groups
    routing, weighting, slot_weight = slot_tables(
        chosen, weights_two, experts, local, CAP, me
    )
    picker = routing.T.astype(BF)
    block = (local, CAP, model)
    rows = local * CAP

    def part(array, d):
        return array[d * rows : (d + 1) * rows]

    def picked(source, d, scale):
        found = jnp.dot(part(picker, d), source, preferred_element_type=F32)
        if scale:
            found = found * part(slot_weight, d)[:, None]
        return found.astype(BF)

    def dispatch(source, scale):
        sent = [picked(source, d, scale) for d in range(groups)]
        got = [sent[0]] + [swap(sent[d], "expert", d) for d in range(1, groups)]
        return jnp.stack([g.reshape(block) for g in got], axis=1).reshape(
            local, groups * CAP, model
        )

    x = dispatch(activations, False)
    c = dispatch(upstream, True)
    gate = dot(x, gate_local, (((2,), (1,)), ((0,), (0,))))
    upper = dot(x, up_local, (((2,), (1,)), ((0,), (0,))))
    sigma = jax.nn.sigmoid(gate)
    hidden = (gate * sigma * upper).astype(BF)
    out = dot(hidden, down_local, (((2,), (1,)), ((0,), (0,)))).astype(BF)
    hidden_cot = dot(c, down_local, (((2,), (2,)), ((0,), (0,))))
    slope = sigma * (1.0 + gate * (1.0 - sigma))
    gate_cot = (hidden_cot * upper * slope).astype(BF)
    up_cot = (hidden_cot * gate * sigma).astype(BF)
    grad = dot(gate_cot, gate_local, (((2,), (2,)), ((0,), (0,))))
    grad = (grad + dot(up_cot, up_local, (((2,), (2,)), ((0,), (0,))))).astype(BF)

    high = weighting.astype(BF)
    low = (weighting - high.astype(F32)).astype(BF)

    def back(values, weighted):
        grid = values.reshape(local, groups, CAP, model)
        total = None
        for d in range(groups):
            piece = grid[:, d].reshape(rows, model)
            if d:
                piece = swap(piece, "expert", d)
            cols = slice(d * rows, (d + 1) * rows)
            if weighted:
                term = dot(
                    jnp.concatenate([high[:, cols], low[:, cols]], axis=1),
                    jnp.concatenate([piece, piece], axis=0),
                    (((1,), (0,)), ((), ())),
                )
            else:
                term = dot(picker[cols].T, piece, (((1,), (0,)), ((), ())))
            total = term if total is None else total + term
        return total.astype(BF)

    outputs = lax.psum(back(out, True), "dp")
    gradient = sum_over(back(grad, False), "dp")
    handed = swap(gradient, "section", 1)
    return (outputs[None], handed[None])


def solution(mesh):
    placed = (
        P("section", "expert", None),
        P("section", "expert", None),
        P("section", "expert", None),
        P("section", "expert", None),
        P("section", "expert", None, "dp"),
        P("section", "expert", None, "dp"),
        P("section", "expert", "dp", None),
    )
    return jax.shard_map(
        body,
        mesh=mesh,
        in_specs=placed,
        out_specs=(P("section", "expert", None), P("section", "expert", None)),
        check_vma=False,
    )
```

```python
import functools

import jax
import jax.numpy as jnp
from jax import lax
from jax.experimental import pallas as pl
from jax.experimental.pallas import tpu as pltpu
from jax.sharding import PartitionSpec as P

CAP = 72
TILE = 512
CHUNKS = 3
PAIR = 896
BF = jnp.bfloat16
F32 = jnp.float32


def swap(block, axis, flip):
    size = lax.axis_size(axis)
    return lax.ppermute(block, axis, [(i, i ^ flip) for i in range(size)])


def slot_tables(chosen, weights_two, experts, local, capacity, me):
    number = chosen.shape[0]
    relative = ((chosen // local) ^ me) * local + chosen % local
    flattened = relative.reshape(-1)
    one_hot = (flattened[:, None] == jnp.arange(experts, dtype=jnp.int32)[None, :]).astype(
        jnp.int32
    )
    earlier = jnp.cumsum(one_hot, axis=0) - one_hot
    position = jnp.sum(earlier * one_hot, axis=1)
    slot_index = flattened * capacity + position
    selection = (
        slot_index[:, None] == jnp.arange(experts * capacity, dtype=jnp.int32)[None, :]
    ).astype(F32)
    selection = selection.reshape(number, 2, experts * capacity)
    routing = jnp.sum(selection, axis=1)
    weighting = jnp.sum(selection * weights_two[:, :, None], axis=1)
    slot_weight = jnp.sum(weighting, axis=0)
    return routing, weighting, slot_weight


def nn(a, b):
    return lax.dot_general(a, b, (((1,), (0,)), ((), ())), preferred_element_type=F32)


def nt(a, b):
    return lax.dot_general(a, b, (((1,), (1,)), ((), ())), preferred_element_type=F32)


def rows_of(arrays):
    return jnp.concatenate([a.astype(F32) for a in arrays], axis=0).astype(BF)


def gather_rows(half_ref, refs, x):
    own = refs[0][0]
    model = own.shape[1]
    pieces = [[r[0] for r in one] for one in refs[1]]
    if len(pieces[0]) == 1:
        x[...] = rows_of([own] + [one[0] for one in pieces])
        return
    direct = pieces[0][0].shape[1]
    width = (model - direct) // 2
    odd = half_ref[0] == 1
    x[:, :direct] = rows_of([own[:, :direct]] + [one[0] for one in pieces])
    low, high = slice(direct, direct + width), slice(direct + width, model)
    pairs = [(one[1].astype(F32), one[2].astype(F32)) for one in pieces]
    x[:, low] = rows_of([own[:, low]] + [jnp.where(odd, b, a) for a, b in pairs])
    x[:, high] = rows_of([own[:, high]] + [jnp.where(odd, a, b) for a, b in pairs])


def hand_out(acc, refs, groups):
    chunks = len(refs) // groups
    width = acc.shape[1] // chunks
    rows = acc.shape[0] // groups
    for g in range(groups):
        for k in range(chunks):
            refs[g * chunks + k][0] = acc[
                g * rows : (g + 1) * rows, k * width : (k + 1) * width
            ].astype(BF)


def grouped(refs, counts):
    found, at = [], 1
    for count in counts:
        found.append(refs[at : at + count])
        at += count
    return refs[0], found


def forward_kernel(counts, half_ref, *refs):
    groups, pieces = 1 + len(counts), 1 + sum(counts)
    wg_ref, wu_ref, wd_ref = refs[pieces : pieces + 3]
    out_refs, (p_ref, q_ref, x, acc) = refs[pieces + 3 : -4], refs[-4:]
    j = pl.program_id(1)

    @pl.when(j == 0)
    def _():
        gather_rows(half_ref, grouped(refs, counts), x)
        acc[...] = jnp.zeros_like(acc)

    gate = nn(x[...], wg_ref[0])
    upper = nn(x[...], wu_ref[0])
    sigma = jax.nn.sigmoid(gate)
    active = gate * sigma
    q_ref[0] = active.astype(BF)
    p_ref[0] = (upper * (sigma * (1.0 + gate * (1.0 - sigma)))).astype(BF)
    acc[...] += nn((active * upper).astype(BF), wd_ref[0])

    @pl.when(j == pl.num_programs(1) - 1)
    def _():
        hand_out(acc, out_refs, groups)


def backward_kernel(counts, half_ref, *refs):
    groups, pieces = 1 + len(counts), 1 + sum(counts)
    p_ref, q_ref, wg_ref, wu_ref, wd_ref = refs[pieces : pieces + 5]
    out_refs, (c, acc) = refs[pieces + 5 : -2], refs[-2:]
    j = pl.program_id(1)

    @pl.when(j == 0)
    def _():
        gather_rows(half_ref, grouped(refs, counts), c)
        acc[...] = jnp.zeros_like(acc)

    hidden_cot = nt(c[...], wd_ref[0])
    gate_cot = (hidden_cot * p_ref[0].astype(F32)).astype(BF)
    up_cot = (hidden_cot * q_ref[0].astype(F32)).astype(BF)
    acc[...] += nt(gate_cot, wg_ref[0]) + nt(up_cot, wu_ref[0])

    @pl.when(j == pl.num_programs(1) - 1)
    def _():
        hand_out(acc, out_refs, groups)


def expert_call(kernel, half, own, others, kept, weights, chunks, keep):
    counts = tuple(len(one) for one in others)
    pieces = [own] + [a for one in others for a in one]
    groups = 1 + len(others)
    local, capacity, model = own.shape
    width = weights[0].shape[2]
    tile = min(TILE, width)
    rows = groups * capacity

    def row_block(columns):
        return pl.BlockSpec((1, capacity, columns), lambda e, j: (e, 0, 0))

    wide = pl.BlockSpec((1, model, tile), lambda e, j: (e, 0, j))
    tall = pl.BlockSpec((1, tile, model), lambda e, j: (e, j, 0))
    act = pl.BlockSpec((1, rows, tile), lambda e, j: (e, 0, j))
    flops = 6 * local * rows * model * width
    return list(
        pl.pallas_call(
            functools.partial(kernel, counts),
            grid=(local, width // tile),
            in_specs=[pl.BlockSpec(memory_space=pltpu.SMEM)]
            + [row_block(a.shape[2]) for a in pieces]
            + [act] * len(kept)
            + [wide, wide, tall],
            out_specs=[row_block(model // chunks)] * (groups * chunks) + [act] * keep,
            out_shape=[jax.ShapeDtypeStruct((local, capacity, model // chunks), BF)]
            * (groups * chunks)
            + [jax.ShapeDtypeStruct((local, rows, width), BF)] * keep,
            scratch_shapes=[pltpu.VMEM((rows, model), BF), pltpu.VMEM((rows, model), F32)],
            compiler_params=pltpu.CompilerParams(vmem_limit_bytes=52 << 20),
            cost_estimate=pl.CostEstimate(
                flops=flops, bytes_accessed=6 * local * model * width, transcendentals=0
            ),
        )(half, *pieces, *kept, *weights)
    )


def sum_over(blocks, axis):
    if lax.axis_size(axis) != 4:
        return [lax.psum(one, axis) for one in blocks]
    z = lax.axis_index(axis)
    middle = (z == 1) | (z == 2)
    count = len(blocks)
    sums, totals, done = {}, {}, []
    for t in range(count + 2):
        sent = totals.get(t - 2) if t >= count else blocks[t]
        if 2 <= t < count:
            sent = jnp.where(middle, totals[t - 2], blocks[t])
        got = swap(sent, axis, 1)
        if 1 <= t <= count:
            crossed = lax.ppermute(sums[t - 1], axis, [(0, 0), (1, 2), (2, 1), (3, 3)])
            totals[t - 1] = (sums[t - 1].astype(F32) + crossed.astype(F32)).astype(BF)
        if t < count:
            sums[t] = (blocks[t].astype(F32) + got.astype(F32)).astype(BF)
        if t >= 2:
            done.append(jnp.where(middle, totals[t - 2], got))
    return done


def body(tokens, expert_ids, gate_probs, cotangent, w_gate, w_up, w_down):
    activations, chosen, weights_two, upstream = tokens[0], expert_ids[0], gate_probs[0], cotangent[0]
    weights = (w_gate[0], w_up[0], w_down[0])
    local, model = weights[0].shape[:2]
    groups = lax.axis_size("expert")
    me = lax.axis_index("expert")
    routing, weighting, slot_weight = slot_tables(
        chosen, weights_two, local * groups, local, CAP, me
    )
    picker = routing.T.astype(BF)
    rows = local * CAP
    part = [slice(d * rows, (d + 1) * rows) for d in range(groups)]

    def exchange(pieces):
        return [pieces[0]] + [swap(pieces[d], "expert", d) for d in range(1, groups)]

    def picked(d, source, scaled):
        found = nn(picker[part[d]], source)
        if scaled:
            found = found * slot_weight[part[d]][:, None]
        return found.astype(BF).reshape(local, CAP, source.shape[1])

    others = range(1, groups)
    half = lax.rem(lax.axis_index("dp"), 2)
    helped = PAIR if model > 2 * PAIR else 0
    direct = model - 2 * helped
    low, high = activations[:, direct : direct + helped], activations[:, direct + helped :]
    fetched = jnp.where(half == 1, high, low)
    near = [swap(picked(d, fetched, False), "expert", d) for d in others]
    straight = [picked(d, activations[:, :direct], False) for d in others]
    near, straight = lax.optimization_barrier((near, straight))
    straight = [swap(straight[d - 1], "expert", d) for d in others]
    far = [swap(one, "dp", 1) for one in near]
    x = [[straight[d], near[d], far[d]] for d in range(groups - 1)]
    c_sent = [picked(d, upstream, True) for d in others]
    x, c_sent = lax.optimization_barrier((x, c_sent))
    c = [[swap(c_sent[d - 1], "expert", d)] for d in others]
    chip_half = half.astype(jnp.int32).reshape(1)
    *out, p, q = expert_call(
        forward_kernel, chip_half, picked(0, activations, False), x, (), weights, 1, 2
    )
    out = exchange(out)
    grad = expert_call(
        backward_kernel, chip_half, picked(0, upstream, True), c, (p, q), weights, CHUNKS, 0
    )

    high = weighting.astype(BF)
    low = (weighting - high.astype(F32)).astype(BF)
    total = 0.0
    for d in range(groups):
        piece = out[d].reshape(rows, model)
        total = total + nn(high[:, part[d]], piece) + nn(low[:, part[d]], piece)
    total = total.astype(BF)
    wide = model // CHUNKS
    blocks = [total[:, k * wide : (k + 1) * wide] for k in range(CHUNKS)]
    later = [grad[d * CHUNKS + k] for d in range(groups) for k in range(1, CHUNKS)]
    blocks, later = lax.optimization_barrier((blocks, later))
    plain = routing.astype(BF)
    for k in range(CHUNKS):
        if k:
            pieces = exchange(later[k - 1 :: CHUNKS - 1])
        else:
            pieces = exchange(grad[0::CHUNKS])
        total = 0.0
        for d in range(groups):
            total = total + nn(plain[:, part[d]], pieces[d].reshape(rows, wide))
        blocks.append(swap(total.astype(BF), "section", 1))
    done = sum_over(blocks, "dp")
    outputs, handed = [jnp.concatenate(done[at : at + CHUNKS], axis=1) for at in (0, CHUNKS)]
    return (outputs[None], handed[None])


def solution(mesh):
    placed = (
        P("section", "expert", None),
        P("section", "expert", None),
        P("section", "expert", None),
        P("section", "expert", None),
        P("section", "expert", None, "dp"),
        P("section", "expert", None, "dp"),
        P("section", "expert", "dp", None),
    )
    return jax.shard_map(
        body,
        mesh=mesh,
        in_specs=placed,
        out_specs=(P("section", "expert", None), P("section", "expert", None)),
        check_vma=False,
    )
```

```python
import functools

import jax
import jax.numpy as jnp
from jax import lax
from jax.experimental import pallas as pl
from jax.experimental.pallas import tpu as pltpu
from jax.sharding import PartitionSpec as P

CAP = 72
TILE = 512
CHUNKS = 3
PAIR = 896
BF = jnp.bfloat16
F32 = jnp.float32


def swap(block, axis, flip):
    size = lax.axis_size(axis)
    return lax.ppermute(block, axis, [(i, i ^ flip) for i in range(size)])


def slot_tables(chosen, weights_two, experts, local, capacity, me):
    number = chosen.shape[0]
    relative = ((chosen // local) ^ me) * local + chosen % local
    flattened = relative.reshape(-1)
    one_hot = (flattened[:, None] == jnp.arange(experts, dtype=jnp.int32)[None, :]).astype(
        jnp.int32
    )
    earlier = jnp.cumsum(one_hot, axis=0) - one_hot
    position = jnp.sum(earlier * one_hot, axis=1)
    slot_index = flattened * capacity + position
    selection = (
        slot_index[:, None] == jnp.arange(experts * capacity, dtype=jnp.int32)[None, :]
    ).astype(F32)
    selection = selection.reshape(number, 2, experts * capacity)
    routing = jnp.sum(selection, axis=1)
    weighting = jnp.sum(selection * weights_two[:, :, None], axis=1)
    slot_weight = jnp.sum(weighting, axis=0)
    return routing, weighting, slot_weight


def nn(a, b):
    return lax.dot_general(a, b, (((1,), (0,)), ((), ())), preferred_element_type=F32)


def nt(a, b):
    return lax.dot_general(a, b, (((1,), (1,)), ((), ())), preferred_element_type=F32)


def rows_of(arrays):
    return jnp.concatenate([a.astype(F32) for a in arrays], axis=0).astype(BF)


def gather_rows(half_ref, refs, x):
    own = refs[0][0]
    model = own.shape[1]
    pieces = [[r[0] for r in one] for one in refs[1]]
    if len(pieces[0]) == 1:
        x[...] = rows_of([own] + [one[0] for one in pieces])
        return
    direct = pieces[0][0].shape[1]
    width = (model - direct) // 2
    odd = half_ref[0] == 1
    x[:, :direct] = rows_of([own[:, :direct]] + [one[0] for one in pieces])
    low, high = slice(direct, direct + width), slice(direct + width, model)
    pairs = [(one[1].astype(F32), one[2].astype(F32)) for one in pieces]
    x[:, low] = rows_of([own[:, low]] + [jnp.where(odd, b, a) for a, b in pairs])
    x[:, high] = rows_of([own[:, high]] + [jnp.where(odd, a, b) for a, b in pairs])


def hand_out(acc, refs, groups):
    chunks = len(refs) // groups
    width = acc.shape[1] // chunks
    rows = acc.shape[0] // groups
    for g in range(groups):
        for k in range(chunks):
            refs[g * chunks + k][0] = acc[
                g * rows : (g + 1) * rows, k * width : (k + 1) * width
            ].astype(BF)


def grouped(refs, counts):
    found, at = [], 1
    for count in counts:
        found.append(refs[at : at + count])
        at += count
    return refs[0], found


def forward_kernel(counts, half_ref, *refs):
    groups, pieces = 1 + len(counts), 1 + sum(counts)
    wg_ref, wu_ref, wd_ref = refs[pieces : pieces + 3]
    out_refs, (p_ref, q_ref, x, acc) = refs[pieces + 3 : -4], refs[-4:]
    j = pl.program_id(1)

    @pl.when(j == 0)
    def _():
        gather_rows(half_ref, grouped(refs, counts), x)
        acc[...] = jnp.zeros_like(acc)

    gate = nn(x[...], wg_ref[0])
    upper = nn(x[...], wu_ref[0])
    sigma = jax.nn.sigmoid(gate)
    active = gate * sigma
    q_ref[0] = active.astype(BF)
    p_ref[0] = (upper * (sigma * (1.0 + gate * (1.0 - sigma)))).astype(BF)
    acc[...] += nn((active * upper).astype(BF), wd_ref[0])

    @pl.when(j == pl.num_programs(1) - 1)
    def _():
        hand_out(acc, out_refs, groups)


def backward_kernel(counts, half_ref, *refs):
    groups, pieces = 1 + len(counts), 1 + sum(counts)
    p_ref, q_ref, wg_ref, wu_ref, wd_ref = refs[pieces : pieces + 5]
    out_refs, (c, acc) = refs[pieces + 5 : -2], refs[-2:]
    j = pl.program_id(1)

    @pl.when(j == 0)
    def _():
        gather_rows(half_ref, grouped(refs, counts), c)
        acc[...] = jnp.zeros_like(acc)

    hidden_cot = nt(c[...], wd_ref[0])
    gate_cot = (hidden_cot * p_ref[0].astype(F32)).astype(BF)
    up_cot = (hidden_cot * q_ref[0].astype(F32)).astype(BF)
    acc[...] += nt(gate_cot, wg_ref[0]) + nt(up_cot, wu_ref[0])

    @pl.when(j == pl.num_programs(1) - 1)
    def _():
        hand_out(acc, out_refs, groups)


def expert_call(kernel, half, own, others, kept, weights, chunks, keep):
    counts = tuple(len(one) for one in others)
    pieces = [own] + [a for one in others for a in one]
    groups = 1 + len(others)
    local, capacity, model = own.shape
    width = weights[0].shape[2]
    tile = min(TILE, width)
    rows = groups * capacity

    def row_block(columns):
        return pl.BlockSpec((1, capacity, columns), lambda e, j: (e, 0, 0))

    wide = pl.BlockSpec((1, model, tile), lambda e, j: (e, 0, j))
    tall = pl.BlockSpec((1, tile, model), lambda e, j: (e, j, 0))
    act = pl.BlockSpec((1, rows, tile), lambda e, j: (e, 0, j))
    flops = 6 * local * rows * model * width
    return list(
        pl.pallas_call(
            functools.partial(kernel, counts),
            grid=(local, width // tile),
            in_specs=[pl.BlockSpec(memory_space=pltpu.SMEM)]
            + [row_block(a.shape[2]) for a in pieces]
            + [act] * len(kept)
            + [wide, wide, tall],
            out_specs=[row_block(model // chunks)] * (groups * chunks) + [act] * keep,
            out_shape=[jax.ShapeDtypeStruct((local, capacity, model // chunks), BF)]
            * (groups * chunks)
            + [jax.ShapeDtypeStruct((local, rows, width), BF)] * keep,
            scratch_shapes=[pltpu.VMEM((rows, model), BF), pltpu.VMEM((rows, model), F32)],
            compiler_params=pltpu.CompilerParams(vmem_limit_bytes=52 << 20),
            cost_estimate=pl.CostEstimate(
                flops=flops, bytes_accessed=6 * local * model * width, transcendentals=0
            ),
        )(half, *pieces, *kept, *weights)
    )


def sum_over(blocks, count, axis, supply):
    if lax.axis_size(axis) != 4:
        for t in range(count):
            supply(t, blocks[0])
        return [lax.psum(one, axis) for one in blocks]
    z = lax.axis_index(axis)
    middle = (z == 1) | (z == 2)
    sums, totals, done = {}, {}, []
    for t in range(count + 2):
        sent = totals.get(t - 2) if t >= count else blocks[t]
        if 2 <= t < count:
            sent = jnp.where(middle, totals[t - 2], blocks[t])
        got = swap(sent, axis, 1)
        if 1 <= t <= count:
            crossed = lax.ppermute(sums[t - 1], axis, [(0, 0), (1, 2), (2, 1), (3, 3)])
            got, crossed = lax.optimization_barrier((got, crossed))
            totals[t - 1] = (sums[t - 1].astype(F32) + crossed.astype(F32)).astype(BF)
        if t < count:
            sums[t] = (blocks[t].astype(F32) + got.astype(F32)).astype(BF)
            sums[t] = supply(t, sums[t])
        if t >= 2:
            done.append(jnp.where(middle, totals[t - 2], got))
    return done


def body(tokens, expert_ids, gate_probs, cotangent, w_gate, w_up, w_down):
    activations, chosen, weights_two, upstream = tokens[0], expert_ids[0], gate_probs[0], cotangent[0]
    weights = (w_gate[0], w_up[0], w_down[0])
    local, model = weights[0].shape[:2]
    groups = lax.axis_size("expert")
    me = lax.axis_index("expert")
    routing, weighting, slot_weight = slot_tables(
        chosen, weights_two, local * groups, local, CAP, me
    )
    picker = routing.T.astype(BF)
    rows = local * CAP
    part = [slice(d * rows, (d + 1) * rows) for d in range(groups)]

    def exchange(pieces):
        return [pieces[0]] + [swap(pieces[d], "expert", d) for d in range(1, groups)]

    def picked(d, source, scaled):
        found = nn(picker[part[d]], source)
        if scaled:
            found = found * slot_weight[part[d]][:, None]
        return found.astype(BF).reshape(local, CAP, source.shape[1])

    others = range(1, groups)
    half = lax.rem(lax.axis_index("dp"), 2)
    helped = PAIR if model > 2 * PAIR else 0
    direct = model - 2 * helped
    low, high = activations[:, direct : direct + helped], activations[:, direct + helped :]
    fetched = jnp.where(half == 1, high, low)
    near = [swap(picked(d, fetched, False), "expert", d) for d in others]
    straight = [picked(d, activations[:, :direct], False) for d in others]
    straight = [swap(straight[d - 1], "expert", d) for d in others]
    far = [swap(one, "dp", 1) for one in near]
    x = [[straight[d], near[d], far[d]] for d in range(groups - 1)]
    c_sent = [picked(d, upstream, True) for d in others]
    c_own = picked(0, upstream, True)
    x, c_sent, c_own = lax.optimization_barrier((x, c_sent, c_own))
    c = [[swap(c_sent[d - 1], "expert", d)] for d in others]
    chip_half = half.astype(jnp.int32).reshape(1)
    *out, p, q = expert_call(
        forward_kernel, chip_half, picked(0, activations, False), x, (), weights, 1, 2
    )
    out = exchange(out)
    grad = expert_call(
        backward_kernel, chip_half, c_own, c, (p, q), weights, CHUNKS, 0
    )

    out[0], grad[0] = lax.optimization_barrier((out[0], grad[0]))
    high = weighting.astype(BF)
    low = (weighting - high.astype(F32)).astype(BF)
    total = 0.0
    for d in range(groups):
        piece = out[d].reshape(rows, model)
        total = total + nn(high[:, part[d]], piece) + nn(low[:, part[d]], piece)
    total = total.astype(BF)
    wide = model // CHUNKS
    blocks = [total[:, k * wide : (k + 1) * wide] for k in range(CHUNKS)]
    plain = routing.astype(BF)

    travelling = exchange(grad[0::CHUNKS])

    def supply(t, arrived):
        nonlocal travelling
        if t < CHUNKS:
            pieces, following, arrived = lax.optimization_barrier(
                (travelling, grad[t + 1 :: CHUNKS] if t + 1 < CHUNKS else [], arrived)
            )
            total = 0.0
            for d in range(groups):
                total = total + nn(plain[:, part[d]], pieces[d].reshape(rows, wide))
            blocks.append(swap(total.astype(BF), "section", 1))
            if following:
                travelling = exchange(following)
        return arrived

    done = sum_over(blocks, 2 * CHUNKS, "dp", supply)
    outputs, handed = [
        jnp.concatenate(done[:CHUNKS], axis=1),
        jnp.concatenate(done[CHUNKS:], axis=1),
    ]
    return (outputs[None], handed[None])


def solution(mesh):
    placed = (
        P("section", "expert", None),
        P("section", "expert", None),
        P("section", "expert", None),
        P("section", "expert", None),
        P("section", "expert", None, "dp"),
        P("section", "expert", None, "dp"),
        P("section", "expert", "dp", None),
    )
    return jax.shard_map(
        body,
        mesh=mesh,
        in_specs=placed,
        out_specs=(P("section", "expert", None), P("section", "expert", None)),
        check_vma=False,
    )
```

```python
import functools

import jax
import jax.numpy as jnp
from jax import lax
from jax.experimental import pallas as pl
from jax.experimental.pallas import tpu as pltpu
from jax.sharding import PartitionSpec as P

CAP = 72
TILE = 512
CHUNKS = 3
PAIR = 896
BF = jnp.bfloat16
F32 = jnp.float32


def swap(block, axis, flip):
    size = lax.axis_size(axis)
    return lax.ppermute(block, axis, [(i, i ^ flip) for i in range(size)])


def slot_tables(chosen, weights_two, experts, local, capacity, me):
    number = chosen.shape[0]
    relative = ((chosen // local) ^ me) * local + chosen % local
    flattened = relative.reshape(-1)
    one_hot = (flattened[:, None] == jnp.arange(experts, dtype=jnp.int32)[None, :]).astype(
        jnp.int32
    )
    earlier = jnp.cumsum(one_hot, axis=0) - one_hot
    position = jnp.sum(earlier * one_hot, axis=1)
    slot_index = flattened * capacity + position
    selection = (
        slot_index[:, None] == jnp.arange(experts * capacity, dtype=jnp.int32)[None, :]
    ).astype(F32)
    selection = selection.reshape(number, 2, experts * capacity)
    routing = jnp.sum(selection, axis=1)
    weighting = jnp.sum(selection * weights_two[:, :, None], axis=1)
    slot_weight = jnp.sum(weighting, axis=0)
    return routing, weighting, slot_weight


def nn(a, b):
    return lax.dot_general(a, b, (((1,), (0,)), ((), ())), preferred_element_type=F32)


def nt(a, b):
    return lax.dot_general(a, b, (((1,), (1,)), ((), ())), preferred_element_type=F32)


def rows_of(arrays):
    return jnp.concatenate([a.astype(F32) for a in arrays], axis=0).astype(BF)


def gather_rows(half_ref, refs, x):
    own = refs[0][0]
    model = own.shape[1]
    pieces = [[r[0] for r in one] for one in refs[1]]
    if len(pieces[0]) == 1:
        x[...] = rows_of([own] + [one[0] for one in pieces])
        return
    direct = pieces[0][0].shape[1]
    width = (model - direct) // 2
    odd = half_ref[0] == 1
    x[:, :direct] = rows_of([own[:, :direct]] + [one[0] for one in pieces])
    low, high = slice(direct, direct + width), slice(direct + width, model)
    pairs = [(one[1].astype(F32), one[2].astype(F32)) for one in pieces]
    x[:, low] = rows_of([own[:, low]] + [jnp.where(odd, b, a) for a, b in pairs])
    x[:, high] = rows_of([own[:, high]] + [jnp.where(odd, a, b) for a, b in pairs])


def hand_out(acc, refs, groups):
    chunks = len(refs) // groups
    width = acc.shape[1] // chunks
    rows = acc.shape[0] // groups
    for g in range(groups):
        for k in range(chunks):
            refs[g * chunks + k][0] = acc[
                g * rows : (g + 1) * rows, k * width : (k + 1) * width
            ].astype(BF)


def grouped(refs, counts):
    found, at = [], 1
    for count in counts:
        found.append(refs[at : at + count])
        at += count
    return refs[0], found


def forward_kernel(counts, half_ref, *refs):
    groups, pieces = 1 + len(counts), 1 + sum(counts)
    wg_ref, wu_ref, wd_ref = refs[pieces : pieces + 3]
    out_refs, (p_ref, q_ref, x, acc) = refs[pieces + 3 : -4], refs[-4:]
    j = pl.program_id(1)

    @pl.when(j == 0)
    def _():
        gather_rows(half_ref, grouped(refs, counts), x)
        acc[...] = jnp.zeros_like(acc)

    gate = nn(x[...], wg_ref[0])
    upper = nn(x[...], wu_ref[0])
    sigma = jax.nn.sigmoid(gate)
    active = gate * sigma
    q_ref[0] = active.astype(BF)
    p_ref[0] = (upper * (sigma * (1.0 + gate * (1.0 - sigma)))).astype(BF)
    acc[...] += nn((active * upper).astype(BF), wd_ref[0])

    @pl.when(j == pl.num_programs(1) - 1)
    def _():
        hand_out(acc, out_refs, groups)


def backward_kernel(counts, half_ref, *refs):
    groups, pieces = 1 + len(counts), 1 + sum(counts)
    p_ref, q_ref, wg_ref, wu_ref, wd_ref = refs[pieces : pieces + 5]
    out_refs, (c, acc) = refs[pieces + 5 : -2], refs[-2:]
    j = pl.program_id(1)

    @pl.when(j == 0)
    def _():
        gather_rows(half_ref, grouped(refs, counts), c)
        acc[...] = jnp.zeros_like(acc)

    hidden_cot = nt(c[...], wd_ref[0])
    gate_cot = (hidden_cot * p_ref[0].astype(F32)).astype(BF)
    up_cot = (hidden_cot * q_ref[0].astype(F32)).astype(BF)
    acc[...] += nt(gate_cot, wg_ref[0]) + nt(up_cot, wu_ref[0])

    @pl.when(j == pl.num_programs(1) - 1)
    def _():
        hand_out(acc, out_refs, groups)


def expert_call(kernel, half, own, others, kept, weights, chunks, keep):
    counts = tuple(len(one) for one in others)
    pieces = [own] + [a for one in others for a in one]
    groups = 1 + len(others)
    local, capacity, model = own.shape
    width = weights[0].shape[2]
    tile = min(TILE, width)
    rows = groups * capacity

    def row_block(columns):
        return pl.BlockSpec((1, capacity, columns), lambda e, j: (e, 0, 0))

    wide = pl.BlockSpec((1, model, tile), lambda e, j: (e, 0, j))
    tall = pl.BlockSpec((1, tile, model), lambda e, j: (e, j, 0))
    act = pl.BlockSpec((1, rows, tile), lambda e, j: (e, 0, j))
    flops = 6 * local * rows * model * width
    return list(
        pl.pallas_call(
            functools.partial(kernel, counts),
            grid=(local, width // tile),
            in_specs=[pl.BlockSpec(memory_space=pltpu.SMEM)]
            + [row_block(a.shape[2]) for a in pieces]
            + [act] * len(kept)
            + [wide, wide, tall],
            out_specs=[row_block(model // chunks)] * (groups * chunks) + [act] * keep,
            out_shape=[jax.ShapeDtypeStruct((local, capacity, model // chunks), BF)]
            * (groups * chunks)
            + [jax.ShapeDtypeStruct((local, rows, width), BF)] * keep,
            scratch_shapes=[pltpu.VMEM((rows, model), BF), pltpu.VMEM((rows, model), F32)],
            compiler_params=pltpu.CompilerParams(vmem_limit_bytes=52 << 20),
            cost_estimate=pl.CostEstimate(
                flops=flops, bytes_accessed=6 * local * model * width, transcendentals=0
            ),
        )(half, *pieces, *kept, *weights)
    )


def sum_over(blocks, count, axis, supply):
    if lax.axis_size(axis) != 4:
        for t in range(count):
            supply(t, blocks[0])
        return [lax.psum(one, axis) for one in blocks]
    z = lax.axis_index(axis)
    middle = (z == 1) | (z == 2)
    sums, totals, done = {}, {}, []
    for t in range(count + 2):
        sent = totals.get(t - 2) if t >= count else blocks[t]
        if 2 <= t < count:
            sent = jnp.where(middle, totals[t - 2], blocks[t])
        got = swap(sent, axis, 1)
        if 1 <= t <= count:
            crossed = lax.ppermute(sums[t - 1], axis, [(0, 0), (1, 2), (2, 1), (3, 3)])
            got, crossed = lax.optimization_barrier((got, crossed))
            totals[t - 1] = (sums[t - 1].astype(F32) + crossed.astype(F32)).astype(BF)
        if t < count:
            sums[t] = (blocks[t].astype(F32) + got.astype(F32)).astype(BF)
            sums[t] = supply(t, sums[t])
        if t >= 2:
            done.append(jnp.where(middle, totals[t - 2], got))
    return done


def body(tokens, expert_ids, gate_probs, cotangent, w_gate, w_up, w_down):
    activations, chosen, weights_two, upstream = tokens[0], expert_ids[0], gate_probs[0], cotangent[0]
    weights = (w_gate[0], w_up[0], w_down[0])
    local, model = weights[0].shape[:2]
    groups = lax.axis_size("expert")
    me = lax.axis_index("expert")
    routing, weighting, slot_weight = slot_tables(
        chosen, weights_two, local * groups, local, CAP, me
    )
    picker = routing.T.astype(BF)
    rows = local * CAP
    part = [slice(d * rows, (d + 1) * rows) for d in range(groups)]

    def exchange(pieces):
        return [pieces[0]] + [swap(pieces[d], "expert", d) for d in range(1, groups)]

    def picked(d, source, scaled):
        found = nn(picker[part[d]], source)
        if scaled:
            found = found * slot_weight[part[d]][:, None]
        return found.astype(BF).reshape(local, CAP, source.shape[1])

    others = range(1, groups)
    half = lax.rem(lax.axis_index("dp"), 2)
    helped = PAIR if model > 2 * PAIR else 0
    direct = model - 2 * helped
    low, high = activations[:, direct : direct + helped], activations[:, direct + helped :]
    fetched = jnp.where(half == 1, high, low)
    near = [swap(picked(d, fetched, False), "expert", d) for d in others]
    straight = [picked(d, activations[:, :direct], False) for d in others]
    straight = [swap(straight[d - 1], "expert", d) for d in others]
    far = [swap(one, "dp", 1) for one in near]
    c_sent = [picked(d, upstream, True) for d in others]
    c_own = picked(0, upstream, True)
    straight, c_sent, c_own = lax.optimization_barrier((straight, c_sent, c_own))
    x = [[straight[d], near[d], far[d]] for d in range(groups - 1)]
    c = [[swap(c_sent[d - 1], "expert", d)] for d in others]
    chip_half = half.astype(jnp.int32).reshape(1)
    *out, p, q = expert_call(
        forward_kernel, chip_half, picked(0, activations, False), x, (), weights, 1, 2
    )
    out = exchange(out)
    grad = expert_call(
        backward_kernel, chip_half, c_own, c, (p, q), weights, CHUNKS, 0
    )

    out[0], grad[0] = lax.optimization_barrier((out[0], grad[0]))
    high = weighting.astype(BF)
    total = 0.0
    for d in range(groups):
        total = total + nn(high[:, part[d]], out[d].reshape(rows, model))
    total = total.astype(BF)
    wide = model // CHUNKS
    blocks = [total[:, k * wide : (k + 1) * wide] for k in range(CHUNKS)]
    plain = routing.astype(BF)

    travelling = exchange(grad[0::CHUNKS])

    def supply(t, arrived):
        nonlocal travelling
        if t < CHUNKS:
            pieces, following, arrived = lax.optimization_barrier(
                (travelling, grad[t + 1 :: CHUNKS] if t + 1 < CHUNKS else [], arrived)
            )
            total = 0.0
            for d in range(groups):
                total = total + nn(plain[:, part[d]], pieces[d].reshape(rows, wide))
            blocks.append(swap(total.astype(BF), "section", 1))
            if following:
                travelling = exchange(following)
        return arrived

    done = sum_over(blocks, 2 * CHUNKS, "dp", supply)
    outputs, handed = [
        jnp.concatenate(done[:CHUNKS], axis=1),
        jnp.concatenate(done[CHUNKS:], axis=1),
    ]
    return (outputs[None], handed[None])


def solution(mesh):
    placed = (
        P("section", "expert", None),
        P("section", "expert", None),
        P("section", "expert", None),
        P("section", "expert", None),
        P("section", "expert", None, "dp"),
        P("section", "expert", None, "dp"),
        P("section", "expert", "dp", None),
    )
    return jax.shard_map(
        body,
        mesh=mesh,
        in_specs=placed,
        out_specs=(P("section", "expert", None), P("section", "expert", None)),
        check_vma=False,
    )
```

```python
import functools

import jax
import jax.numpy as jnp
from jax import lax
from jax.experimental import pallas as pl
from jax.experimental.pallas import tpu as pltpu
from jax.sharding import PartitionSpec as P

CAP = 72
TILE = 512
CHUNKS = 3
PAIR = 896
BF = jnp.bfloat16
F32 = jnp.float32


def swap(block, axis, flip):
    size = lax.axis_size(axis)
    return lax.ppermute(block, axis, [(i, i ^ flip) for i in range(size)])


def slot_tables(chosen, weights_two, experts, local, capacity, me):
    number = chosen.shape[0]
    relative = ((chosen // local) ^ me) * local + chosen % local
    flattened = relative.reshape(-1)
    one_hot = (flattened[:, None] == jnp.arange(experts, dtype=jnp.int32)[None, :]).astype(
        jnp.int32
    )
    earlier = jnp.cumsum(one_hot, axis=0) - one_hot
    position = jnp.sum(earlier * one_hot, axis=1)
    slot_index = flattened * capacity + position
    selection = (
        slot_index[:, None] == jnp.arange(experts * capacity, dtype=jnp.int32)[None, :]
    ).astype(F32)
    selection = selection.reshape(number, 2, experts * capacity)
    routing = jnp.sum(selection, axis=1)
    weighting = jnp.sum(selection * weights_two[:, :, None], axis=1)
    slot_weight = jnp.sum(weighting, axis=0)
    return routing, weighting, slot_weight


def nn(a, b):
    return lax.dot_general(a, b, (((1,), (0,)), ((), ())), preferred_element_type=F32)


def nt(a, b):
    return lax.dot_general(a, b, (((1,), (1,)), ((), ())), preferred_element_type=F32)


def rows_of(arrays):
    return jnp.concatenate([a.astype(F32) for a in arrays], axis=0).astype(BF)


def gather_rows(half_ref, refs, x):
    own = refs[0][0]
    model = own.shape[1]
    pieces = [[r[0] for r in one] for one in refs[1]]
    if len(pieces[0]) == 1:
        x[...] = rows_of([own] + [one[0] for one in pieces])
        return
    direct = pieces[0][0].shape[1]
    width = (model - direct) // 2
    odd = half_ref[0] == 1
    x[:, :direct] = rows_of([own[:, :direct]] + [one[0] for one in pieces])
    low, high = slice(direct, direct + width), slice(direct + width, model)
    pairs = [(one[1].astype(F32), one[2].astype(F32)) for one in pieces]
    x[:, low] = rows_of([own[:, low]] + [jnp.where(odd, b, a) for a, b in pairs])
    x[:, high] = rows_of([own[:, high]] + [jnp.where(odd, a, b) for a, b in pairs])


def hand_out(acc, refs, groups):
    chunks = len(refs) // groups
    width = acc.shape[1] // chunks
    rows = acc.shape[0] // groups
    for g in range(groups):
        for k in range(chunks):
            refs[g * chunks + k][0] = acc[
                g * rows : (g + 1) * rows, k * width : (k + 1) * width
            ].astype(BF)


def grouped(refs, counts):
    found, at = [], 1
    for count in counts:
        found.append(refs[at : at + count])
        at += count
    return refs[0], found


def forward_kernel(counts, half_ref, *refs):
    groups, pieces = 1 + len(counts), 1 + sum(counts)
    wg_ref, wu_ref, wd_ref = refs[pieces : pieces + 3]
    out_refs, (p_ref, q_ref, x, acc) = refs[pieces + 3 : -4], refs[-4:]
    j = pl.program_id(1)

    @pl.when(j == 0)
    def _():
        gather_rows(half_ref, grouped(refs, counts), x)
        acc[...] = jnp.zeros_like(acc)

    gate = nn(x[...], wg_ref[0])
    upper = nn(x[...], wu_ref[0])
    sigma = jax.nn.sigmoid(gate)
    active = gate * sigma
    q_ref[0] = active.astype(BF)
    p_ref[0] = (upper * (sigma * (1.0 + gate * (1.0 - sigma)))).astype(BF)
    acc[...] += nn((active * upper).astype(BF), wd_ref[0])

    @pl.when(j == pl.num_programs(1) - 1)
    def _():
        hand_out(acc, out_refs, groups)


def backward_kernel(counts, half_ref, *refs):
    groups, pieces = 1 + len(counts), 1 + sum(counts)
    p_ref, q_ref, wg_ref, wu_ref, wd_ref = refs[pieces : pieces + 5]
    out_refs, (c, acc) = refs[pieces + 5 : -2], refs[-2:]
    j = pl.program_id(1)

    @pl.when(j == 0)
    def _():
        gather_rows(half_ref, grouped(refs, counts), c)
        acc[...] = jnp.zeros_like(acc)

    hidden_cot = nt(c[...], wd_ref[0])
    gate_cot = (hidden_cot * p_ref[0].astype(F32)).astype(BF)
    up_cot = (hidden_cot * q_ref[0].astype(F32)).astype(BF)
    acc[...] += nt(gate_cot, wg_ref[0]) + nt(up_cot, wu_ref[0])

    @pl.when(j == pl.num_programs(1) - 1)
    def _():
        hand_out(acc, out_refs, groups)


def expert_call(kernel, half, own, others, kept, weights, chunks, keep):
    counts = tuple(len(one) for one in others)
    pieces = [own] + [a for one in others for a in one]
    groups = 1 + len(others)
    local, capacity, model = own.shape
    width = weights[0].shape[2]
    tile = min(TILE, width)
    rows = groups * capacity

    def row_block(columns):
        return pl.BlockSpec((1, capacity, columns), lambda e, j: (e, 0, 0))

    wide = pl.BlockSpec((1, model, tile), lambda e, j: (e, 0, j))
    tall = pl.BlockSpec((1, tile, model), lambda e, j: (e, j, 0))
    act = pl.BlockSpec((1, rows, tile), lambda e, j: (e, 0, j))
    flops = 6 * local * rows * model * width
    return list(
        pl.pallas_call(
            functools.partial(kernel, counts),
            grid=(local, width // tile),
            in_specs=[pl.BlockSpec(memory_space=pltpu.SMEM)]
            + [row_block(a.shape[2]) for a in pieces]
            + [act] * len(kept)
            + [wide, wide, tall],
            out_specs=[row_block(model // chunks)] * (groups * chunks) + [act] * keep,
            out_shape=[jax.ShapeDtypeStruct((local, capacity, model // chunks), BF)]
            * (groups * chunks)
            + [jax.ShapeDtypeStruct((local, rows, width), BF)] * keep,
            scratch_shapes=[pltpu.VMEM((rows, model), BF), pltpu.VMEM((rows, model), F32)],
            compiler_params=pltpu.CompilerParams(vmem_limit_bytes=52 << 20),
            cost_estimate=pl.CostEstimate(
                flops=flops, bytes_accessed=6 * local * model * width, transcendentals=0
            ),
        )(half, *pieces, *kept, *weights)
    )


def sum_over(blocks, count, axis, supply):
    if lax.axis_size(axis) != 4:
        for t in range(count):
            supply(t, blocks[0])
        return [lax.psum(one, axis) for one in blocks]
    z = lax.axis_index(axis)
    middle = (z == 1) | (z == 2)
    sums, totals, done = {}, {}, []
    for t in range(count + 2):
        sent = totals.get(t - 2) if t >= count else blocks[t]
        if 2 <= t < count:
            sent = jnp.where(middle, totals[t - 2], blocks[t])
        got = swap(sent, axis, 1)
        if 1 <= t <= count:
            crossed = lax.ppermute(sums[t - 1], axis, [(0, 0), (1, 2), (2, 1), (3, 3)])
            got, crossed = lax.optimization_barrier((got, crossed))
            totals[t - 1] = (sums[t - 1].astype(F32) + crossed.astype(F32)).astype(BF)
        if t < count:
            sums[t] = (blocks[t].astype(F32) + got.astype(F32)).astype(BF)
            sums[t] = supply(t, sums[t])
        if t >= 2:
            done.append(jnp.where(middle, totals[t - 2], got))
    return done


def body(tokens, expert_ids, gate_probs, cotangent, w_gate, w_up, w_down):
    activations, chosen, weights_two, upstream = tokens[0], expert_ids[0], gate_probs[0], cotangent[0]
    weights = (w_gate[0], w_up[0], w_down[0])
    local, model = weights[0].shape[:2]
    groups = lax.axis_size("expert")
    me = lax.axis_index("expert")
    routing, weighting, slot_weight = slot_tables(
        chosen, weights_two, local * groups, local, CAP, me
    )
    picker = routing.T.astype(BF)
    rows = local * CAP
    part = [slice(d * rows, (d + 1) * rows) for d in range(groups)]

    def exchange(pieces):
        return [pieces[0]] + [swap(pieces[d], "expert", d) for d in range(1, groups)]

    def picked(d, source, scaled):
        found = nn(picker[part[d]], source)
        if scaled:
            found = found * slot_weight[part[d]][:, None]
        return found.astype(BF).reshape(local, CAP, source.shape[1])

    others = range(1, groups)
    half = lax.rem(lax.axis_index("dp"), 2)
    helped = PAIR if model > 2 * PAIR else 0
    direct = model - 2 * helped
    fetched = lax.dynamic_slice_in_dim(activations, direct + half * helped, helped, axis=1)
    near = [swap(picked(d, fetched, False), "expert", d) for d in others]
    straight = [picked(d, activations[:, :direct], False) for d in others]
    straight = [swap(straight[d - 1], "expert", d) for d in others]
    far = [swap(one, "dp", 1) for one in near]
    c_sent = [picked(d, upstream, True) for d in others]
    c_own = picked(0, upstream, True)
    straight, c_sent, c_own = lax.optimization_barrier((straight, c_sent, c_own))
    x = [[straight[d], near[d], far[d]] for d in range(groups - 1)]
    c = [[swap(c_sent[d - 1], "expert", d)] for d in others]
    chip_half = half.astype(jnp.int32).reshape(1)
    *out, p, q = expert_call(
        forward_kernel, chip_half, picked(0, activations, False), x, (), weights, 1, 2
    )
    out = exchange(out)
    grad = expert_call(
        backward_kernel, chip_half, c_own, c, (p, q), weights, CHUNKS, 0
    )

    out[0], grad[0] = lax.optimization_barrier((out[0], grad[0]))
    high = weighting.astype(BF)
    total = 0.0
    for d in range(groups):
        total = total + nn(high[:, part[d]], out[d].reshape(rows, model))
    total = total.astype(BF)
    wide = model // CHUNKS
    blocks = [total[:, k * wide : (k + 1) * wide] for k in range(CHUNKS)]
    plain = routing.astype(BF)

    travelling = {0: exchange(grad[0::CHUNKS])}

    def supply(t, arrived):
        if 1 <= t <= CHUNKS:
            last, arrived = lax.optimization_barrier((travelling[t - 1][-1], arrived))
            pieces = travelling[t - 1][:-1] + [last]
            total = 0.0
            for d in range(groups):
                total = total + nn(plain[:, part[d]], pieces[d].reshape(rows, wide))
            blocks.append(swap(total.astype(BF), "section", 1))
        if t < CHUNKS:
            following = grad[t + 1 :: CHUNKS] if t + 1 < CHUNKS else []
            travelling[t][:-1], following, arrived = lax.optimization_barrier(
                (travelling[t][:-1], following, arrived)
            )
            if following:
                travelling[t + 1] = exchange(following)
        return arrived

    done = sum_over(blocks, 2 * CHUNKS, "dp", supply)
    outputs, handed = [
        jnp.concatenate(done[:CHUNKS], axis=1),
        jnp.concatenate(done[CHUNKS:], axis=1),
    ]
    return (outputs[None], handed[None])


def solution(mesh):
    placed = (
        P("section", "expert", None),
        P("section", "expert", None),
        P("section", "expert", None),
        P("section", "expert", None),
        P("section", "expert", None, "dp"),
        P("section", "expert", None, "dp"),
        P("section", "expert", "dp", None),
    )
    return jax.shard_map(
        body,
        mesh=mesh,
        in_specs=placed,
        out_specs=(P("section", "expert", None), P("section", "expert", None)),
        check_vma=False,
    )
```

```python
import functools

import jax
import jax.numpy as jnp
from jax import lax
from jax.experimental import pallas as pl
from jax.experimental.pallas import tpu as pltpu
from jax.sharding import PartitionSpec as P

CAP = 72
TILE = 512
CHUNKS = 3
PAIR = 896
BF = jnp.bfloat16
F32 = jnp.float32


def swap(block, axis, flip):
    size = lax.axis_size(axis)
    return lax.ppermute(block, axis, [(i, i ^ flip) for i in range(size)])


def slot_tables(chosen, weights_two, experts, local, capacity, me):
    number = chosen.shape[0]
    relative = (((chosen // local) ^ me) * local + chosen % local).T
    numbers = jnp.arange(experts, dtype=jnp.int32)[:, None]
    first, second = relative[0:1] == numbers, relative[1:2] == numbers
    member = first | second
    token = jnp.arange(number, dtype=jnp.int32)
    before = (token[:, None] < token[None, :]).astype(BF)
    place = nn(member.astype(BF), before).astype(jnp.int32)
    place = jnp.where(member, place, -1)
    slots = jnp.arange(capacity, dtype=jnp.int32)[None, :, None]
    routing = (place[:, None, :] == slots).astype(F32)
    weight = jnp.where(first, weights_two[:, 0][None, :], 0.0)
    weight = weight + jnp.where(second, weights_two[:, 1][None, :], 0.0)
    weighting = (routing * weight[:, None, :]).reshape(experts * capacity, number)
    return routing.reshape(experts * capacity, number), weighting, jnp.sum(weighting, axis=1)


def nn(a, b):
    return lax.dot_general(a, b, (((1,), (0,)), ((), ())), preferred_element_type=F32)


def nt(a, b):
    return lax.dot_general(a, b, (((1,), (1,)), ((), ())), preferred_element_type=F32)


def rows_of(arrays):
    return jnp.concatenate([a.astype(F32) for a in arrays], axis=0).astype(BF)


def gather_rows(half_ref, refs, x):
    own = refs[0][0]
    model = own.shape[1]
    pieces = [[r[0] for r in one] for one in refs[1]]
    if len(pieces[0]) == 1:
        x[...] = rows_of([own] + [one[0] for one in pieces])
        return
    direct = pieces[0][0].shape[1]
    width = (model - direct) // 2
    odd = half_ref[0] == 1
    x[:, :direct] = rows_of([own[:, :direct]] + [one[0] for one in pieces])
    low, high = slice(direct, direct + width), slice(direct + width, model)
    pairs = [(one[1].astype(F32), one[2].astype(F32)) for one in pieces]
    x[:, low] = rows_of([own[:, low]] + [jnp.where(odd, b, a) for a, b in pairs])
    x[:, high] = rows_of([own[:, high]] + [jnp.where(odd, a, b) for a, b in pairs])


def hand_out(acc, refs, groups):
    chunks = len(refs) // groups
    width = acc.shape[1] // chunks
    rows = acc.shape[0] // groups
    for g in range(groups):
        for k in range(chunks):
            refs[g * chunks + k][0] = acc[
                g * rows : (g + 1) * rows, k * width : (k + 1) * width
            ].astype(BF)


def grouped(refs, counts):
    found, at = [], 1
    for count in counts:
        found.append(refs[at : at + count])
        at += count
    return refs[0], found


def forward_kernel(counts, half_ref, *refs):
    groups, pieces = 1 + len(counts), 1 + sum(counts)
    wg_ref, wu_ref, wd_ref = refs[pieces : pieces + 3]
    out_refs, (p_ref, q_ref, x, acc) = refs[pieces + 3 : -4], refs[-4:]
    j = pl.program_id(1)

    @pl.when(j == 0)
    def _():
        gather_rows(half_ref, grouped(refs, counts), x)
        acc[...] = jnp.zeros_like(acc)

    gate = nn(x[...], wg_ref[0])
    upper = nn(x[...], wu_ref[0])
    sigma = jax.nn.sigmoid(gate)
    active = gate * sigma
    q_ref[0] = active.astype(BF)
    p_ref[0] = (upper * (sigma * (1.0 + gate * (1.0 - sigma)))).astype(BF)
    acc[...] += nn((active * upper).astype(BF), wd_ref[0])

    @pl.when(j == pl.num_programs(1) - 1)
    def _():
        hand_out(acc, out_refs, groups)


def backward_kernel(counts, half_ref, *refs):
    groups, pieces = 1 + len(counts), 1 + sum(counts)
    p_ref, q_ref, wg_ref, wu_ref, wd_ref = refs[pieces : pieces + 5]
    out_refs, (c, acc) = refs[pieces + 5 : -2], refs[-2:]
    j = pl.program_id(1)

    @pl.when(j == 0)
    def _():
        gather_rows(half_ref, grouped(refs, counts), c)
        acc[...] = jnp.zeros_like(acc)

    hidden_cot = nt(c[...], wd_ref[0])
    gate_cot = (hidden_cot * p_ref[0].astype(F32)).astype(BF)
    up_cot = (hidden_cot * q_ref[0].astype(F32)).astype(BF)
    acc[...] += nt(gate_cot, wg_ref[0]) + nt(up_cot, wu_ref[0])

    @pl.when(j == pl.num_programs(1) - 1)
    def _():
        hand_out(acc, out_refs, groups)


def expert_call(kernel, half, own, others, kept, weights, chunks, keep):
    counts = tuple(len(one) for one in others)
    pieces = [own] + [a for one in others for a in one]
    groups = 1 + len(others)
    local, capacity, model = own.shape
    width = weights[0].shape[2]
    tile = min(TILE, width)
    rows = groups * capacity

    def row_block(columns):
        return pl.BlockSpec((1, capacity, columns), lambda e, j: (e, 0, 0))

    wide = pl.BlockSpec((1, model, tile), lambda e, j: (e, 0, j))
    tall = pl.BlockSpec((1, tile, model), lambda e, j: (e, j, 0))
    act = pl.BlockSpec((1, rows, tile), lambda e, j: (e, 0, j))
    flops = 6 * local * rows * model * width
    return list(
        pl.pallas_call(
            functools.partial(kernel, counts),
            grid=(local, width // tile),
            in_specs=[pl.BlockSpec(memory_space=pltpu.SMEM)]
            + [row_block(a.shape[2]) for a in pieces]
            + [act] * len(kept)
            + [wide, wide, tall],
            out_specs=[row_block(model // chunks)] * (groups * chunks) + [act] * keep,
            out_shape=[jax.ShapeDtypeStruct((local, capacity, model // chunks), BF)]
            * (groups * chunks)
            + [jax.ShapeDtypeStruct((local, rows, width), BF)] * keep,
            scratch_shapes=[pltpu.VMEM((rows, model), BF), pltpu.VMEM((rows, model), F32)],
            compiler_params=pltpu.CompilerParams(vmem_limit_bytes=52 << 20),
            cost_estimate=pl.CostEstimate(
                flops=flops, bytes_accessed=6 * local * model * width, transcendentals=0
            ),
        )(half, *pieces, *kept, *weights)
    )


def sum_over(blocks, count, axis, supply):
    if lax.axis_size(axis) != 4:
        for t in range(count):
            supply(t, blocks[0])
        return [lax.psum(one, axis) for one in blocks]
    z = lax.axis_index(axis)
    middle = (z == 1) | (z == 2)
    sums, totals, done = {}, {}, []
    for t in range(count + 2):
        sent = totals.get(t - 2) if t >= count else blocks[t]
        if 2 <= t < count:
            sent = jnp.where(middle, totals[t - 2], blocks[t])
        got = swap(sent, axis, 1)
        if 1 <= t <= count:
            crossed = lax.ppermute(sums[t - 1], axis, [(0, 0), (1, 2), (2, 1), (3, 3)])
            got, crossed = lax.optimization_barrier((got, crossed))
            totals[t - 1] = (sums[t - 1].astype(F32) + crossed.astype(F32)).astype(BF)
        if t < count:
            sums[t] = (blocks[t].astype(F32) + got.astype(F32)).astype(BF)
            sums[t] = supply(t, sums[t])
        if t >= 2:
            done.append(jnp.where(middle, totals[t - 2], got))
    return done


def body(tokens, expert_ids, gate_probs, cotangent, w_gate, w_up, w_down):
    activations, chosen, weights_two, upstream = tokens[0], expert_ids[0], gate_probs[0], cotangent[0]
    weights = (w_gate[0], w_up[0], w_down[0])
    local, model = weights[0].shape[:2]
    groups = lax.axis_size("expert")
    me = lax.axis_index("expert")
    routing, weighting, slot_weight = slot_tables(
        chosen, weights_two, local * groups, local, CAP, me
    )
    picker = lax.optimization_barrier(routing.astype(BF))
    rows = local * CAP
    part = [slice(d * rows, (d + 1) * rows) for d in range(groups)]

    def exchange(pieces):
        return [pieces[0]] + [swap(pieces[d], "expert", d) for d in range(1, groups)]

    def picked(d, source, scaled):
        found = nn(picker[part[d]], source)
        if scaled:
            found = found * slot_weight[part[d]][:, None]
        return found.astype(BF).reshape(local, CAP, source.shape[1])

    others = range(1, groups)
    half = lax.rem(lax.axis_index("dp"), 2)
    helped = PAIR if model > 2 * PAIR else 0
    direct = model - 2 * helped
    fetched = lax.dynamic_slice_in_dim(activations, direct + half * helped, helped, axis=1)
    near = [swap(picked(d, fetched, False), "expert", d) for d in others]
    straight = [picked(d, activations[:, :direct], False) for d in others]
    straight = [swap(straight[d - 1], "expert", d) for d in others]
    far = [swap(one, "dp", 1) for one in near]
    c_sent = [picked(d, upstream, True) for d in others]
    c_own = picked(0, upstream, True)
    plain, high = picker.T, weighting.T.astype(BF)
    straight, c_sent, c_own, plain, high = lax.optimization_barrier(
        (straight, c_sent, c_own, plain, high)
    )
    x = [[straight[d], near[d], far[d]] for d in range(groups - 1)]
    c = [[swap(c_sent[d - 1], "expert", d)] for d in others]
    chip_half = half.astype(jnp.int32).reshape(1)
    *out, p, q = expert_call(
        forward_kernel, chip_half, picked(0, activations, False), x, (), weights, 1, 2
    )
    out = exchange(out)
    grad = expert_call(
        backward_kernel, chip_half, c_own, c, (p, q), weights, CHUNKS, 0
    )

    out[0], grad[0] = lax.optimization_barrier((out[0], grad[0]))
    total = 0.0
    for d in range(groups):
        total = total + nn(high[:, part[d]], out[d].reshape(rows, model))
    total = total.astype(BF)
    wide = model // CHUNKS
    blocks = [total[:, k * wide : (k + 1) * wide] for k in range(CHUNKS)]

    travelling = {0: exchange(grad[0::CHUNKS])}

    def supply(t, arrived):
        if 1 <= t <= CHUNKS:
            last, arrived = lax.optimization_barrier((travelling[t - 1][-1], arrived))
            pieces = travelling[t - 1][:-1] + [last]
            total = 0.0
            for d in range(groups):
                total = total + nn(plain[:, part[d]], pieces[d].reshape(rows, wide))
            blocks.append(swap(total.astype(BF), "section", 1))
        if t < CHUNKS:
            following = grad[t + 1 :: CHUNKS] if t + 1 < CHUNKS else []
            travelling[t][:-1], following, arrived = lax.optimization_barrier(
                (travelling[t][:-1], following, arrived)
            )
            if following:
                travelling[t + 1] = exchange(following)
        return arrived

    done = sum_over(blocks, 2 * CHUNKS, "dp", supply)
    outputs, handed = [
        jnp.concatenate(done[:CHUNKS], axis=1),
        jnp.concatenate(done[CHUNKS:], axis=1),
    ]
    return (outputs[None], handed[None])


def solution(mesh):
    placed = (
        P("section", "expert", None),
        P("section", "expert", None),
        P("section", "expert", None),
        P("section", "expert", None),
        P("section", "expert", None, "dp"),
        P("section", "expert", None, "dp"),
        P("section", "expert", "dp", None),
    )
    return jax.shard_map(
        body,
        mesh=mesh,
        in_specs=placed,
        out_specs=(P("section", "expert", None), P("section", "expert", None)),
        check_vma=False,
    )
```
